32 devices in a mesh: grp: 2 (over y), slab: 2 (over x), lat: 8 (over z, core).
Axes of the slice: x: 2, y: 2, z: 4, core: 2. Of those that a mesh axis runs over, the one named last changes fastest.
Arguments:
- cond_lists: int32 [64, 16], P(('slab', 'lat')), may hold values from 0 to 31, all different within a row
- regress: float32 [64, 128, 2048], P(('slab', 'lat')), may hold values from -0.09375 to 0.09375
- chol: float32 [64, 128, 128], P(('slab', 'lat')), as said below
- noise: float32 [128, 256, 128], P(('grp', 'slab', 'lat')), parts along dimension 0, may hold values from -6 to 6
- start_field: float32 [64, 256, 128], P(('grp', 'lat')), parts along dimension 0, may hold values from -6 to 6
Outputs:
- field: float32 [128, 256, 128], P(('grp', 'slab', 'lat')), parts along dimension 0
The draws below stay inside these ranges and needn't reach their ends.
There are 2 independent parts, one for each index of `grp`. The reference program is written for one: setup_inputs(seed, part) draws one part's arguments, and reference() takes and returns one part's arrays. A program takes and returns all parts, laid end to end along the dimension named above; an argument that names none is the same for every part. Nothing has to cross between parts.
Inputs may be any that keep to these rules, and one draw needn't show every extreme that they name: `cond_lists`: each row names 16 distinct positions of the previous slab. `chol`: each factor is lower triangular with diagonal entries from 0.3 to 0.7.
All inputs are finite; a program needn't handle non-finite values.
Results may differ from the reference program's by a relative error of at most 0.0001.
Values sent between devices are 32-bit elements; how exact they have to be, the bound alone decides.
A program may use at most 64 MiB of HBM per device.

```python
import math
import jax
import jax.numpy as jnp
from jax import lax

B = 128
K = 16
BD = 4
NREAL = 256
NBLK = 64
N_SLAB = 2
N_LAT = 8


def draw_chol(key, part):
    off_key = jax.random.fold_in(key, 11)
    diag_key = jax.random.fold_in(key, 23)
    row_index = jnp.arange(B)
    below_mask = (row_index[:, None] > row_index[None, :]).astype(jnp.float32)
    spread = jax.random.normal(off_key, (NBLK, B, B), jnp.float32)
    diagonal = jax.random.uniform(diag_key, (NBLK, B), jnp.float32, 0.3, 0.7)
    return spread * below_mask / math.sqrt(2.0 * B) + diagonal[:, :, None] * jnp.eye(B, dtype=jnp.float32)


def steps_of(own_key, shape, split, least, high):
    def one(axis_at, blocks):
        heights = jax.random.uniform(jax.random.fold_in(jax.random.fold_in(own_key, 6), axis_at), (blocks,), jnp.float32, least / len(split), high / len(split))
        return jnp.repeat(jnp.exp(heights), shape[axis_at] // blocks).reshape((-1,) + (1,) * (len(shape) - axis_at - 1))

    level = one(*split[0])
    for cut in split[1:]:
        level = level * one(*cut)
    return level


def picks_of(key, rows, count, top, lift):
    ranking = jax.random.permutation(jax.random.fold_in(key, 1), count)
    pull = ranking
    for power in range(3):
        pull = pull * pull // count
    pull = pull * lift // count
    chance = jax.random.randint(jax.random.fold_in(key, 2), (rows, count), 0, 4096) + pull
    holders = jax.random.permutation(jax.random.fold_in(key, 3), rows)[jnp.arange(count) % rows]
    chance = jnp.where(jnp.arange(rows)[:, None] == holders[None, :], 1 << 14, chance)
    merit = chance * count + jnp.arange(count)
    return lax.top_k(merit.astype(jnp.int32), top)[1].astype(jnp.int32)


def centred(own_key, extent, scale, limit, shards=(), kind=jnp.bfloat16):
    drawn = scale * jax.random.normal(own_key, extent, jnp.float32)
    if shards:
        drawn = drawn * steps_of(own_key, extent, shards, -0.22, 0.18)
    return jnp.clip(drawn, -limit, limit).astype(kind)


def setup_inputs(seed: int = 0, part: int = 0) -> dict:
    key_list = jax.random.split(jax.random.key(seed), 6)
    part_splits = jax.random.split(jax.random.fold_in(key_list[5], part), 6)
    cond_lists = picks_of(key_list[0], NBLK, N_LAT * BD, K, 8192)
    regress = centred(key_list[1], (NBLK, B, K * B), (2 * K * B) ** -0.5, 0.09375, ((0, 16),), jnp.float32)
    chol = draw_chol(jax.random.fold_in(key_list[5], 71), part)
    noise = centred(part_splits[3], (NBLK, NREAL, B), 1.0, 6.0, ((0, 16),), jnp.float32)
    start_field = centred(part_splits[4], (N_LAT * BD, NREAL, B), 1.0, 6.0, ((0, 8),), jnp.float32)
    return dict(cond_lists=cond_lists, regress=regress, chol=chol, noise=noise, start_field=start_field)


def reference(cond_lists, regress, chol, noise, start_field):
    per_slab = N_LAT * BD
    previous = start_field
    pieces = []
    for slab_step in range(N_SLAB):
        lower_edge = slab_step * per_slab
        lists_here = cond_lists[lower_edge:lower_edge + per_slab]
        factors = regress[lower_edge:lower_edge + per_slab].reshape(per_slab, B, K, B)
        picked = previous[lists_here]
        mean_part = jnp.einsum("jakb,jkwb->jwa", factors, picked, precision=lax.Precision.HIGHEST)
        shock_part = jnp.einsum("jab,jwb->jwa", chol[lower_edge:lower_edge + per_slab], noise[lower_edge:lower_edge + per_slab], precision=lax.Precision.HIGHEST)
        fresh_blocks = mean_part + shock_part
        pieces.append(fresh_blocks)
        previous = fresh_blocks
    return jnp.concatenate(pieces, 0)
```

```python
import functools

import jax
import jax.numpy as jnp
from jax import lax
from jax.experimental import pallas as pl
from jax.experimental.pallas import tpu as pltpu
from jax.sharding import PartitionSpec as P

MESH = pl.DeviceIdType.MESH
FRONT = 32
LEAD = 2


def halves(x):
    high = x.astype(jnp.bfloat16)
    low = (x - high.astype(jnp.float32)).astype(jnp.bfloat16)
    return high, low


def folded(product, rows, columns):
    small = product[:rows, columns:] + product[rows:, :columns] + product[rows:, columns:]
    return product[:rows, :columns] + small


def kernel(
    n_slab, n_lat, front,
    cond, regress_hbm, chol_ref, noise_ref, start_hbm, out_ref,
    held, factors, weights, split,
    start_sem, factor_sem,
    lane_send, lane_recv, end_send, pair_send, pair_recv, slab_send, slab_recv,
):
    blocks, nreal, size = noise_ref.shape
    listed = regress_hbm.shape[2] // size
    fronts = nreal // front
    chips = n_lat // 2
    slab = lax.axis_index("slab")
    lat = lax.axis_index("lat")
    chip, core = lax.div(lat, 2), lax.rem(lat, 2)
    first, last = slab == 0, slab == n_slab - 1

    def lat_of(other_chip, other_core):
        return other_chip * 2 + other_core

    def chunk(f, of_lat):
        return held.at[f, pl.ds(of_lat * blocks, blocks)]

    def start_copy(f):
        return pltpu.make_async_copy(
            start_hbm.at[:, pl.ds(f * front, front)], chunk(f, lat), start_sem.at[f]
        )

    def factor_copy(j):
        return pltpu.make_async_copy(regress_hbm.at[j], factors.at[j], factor_sem.at[j])

    @pl.when(first)
    def _():
        for f in range(fronts):
            start_copy(f).start()

    for j in range(blocks):
        factor_copy(j).start()

    barrier = pltpu.get_barrier_semaphore()

    def greet(**where):
        pl.semaphore_signal(barrier, inc=1, device_id=where, device_id_type=MESH)

    for o in range(1, chips):
        greet(lat=lat_of(lax.rem(chip + o, chips), core))
    greet(lat=lat_of(chip, 1 - core))

    @pl.when(jnp.logical_not(first))
    def _():
        greet(slab=slab - 1)

    @pl.when(jnp.logical_not(last))
    def _():
        greet(slab=slab + 1)

    partners = chips + jnp.where(first, 0, 1) + jnp.where(last, 0, 1)
    pl.semaphore_wait(barrier, partners)

    def lane_copy(f, o):
        return pltpu.make_async_remote_copy(
            src_ref=chunk(f, lat), dst_ref=chunk(f, lat),
            send_sem=lane_send.at[f, o], recv_sem=lane_recv.at[f, o],
            device_id={"lat": lat_of(lax.rem(chip + o, chips), core)}, device_id_type=MESH,
        )

    def lane_arrival(f, o):
        source = lat_of(lax.rem(chip + chips - o, chips), core)
        return pltpu.make_async_remote_copy(
            src_ref=chunk(f, source), dst_ref=chunk(f, source),
            send_sem=lane_send.at[f, o], recv_sem=lane_recv.at[f, o],
            device_id={"lat": lat_of(lax.rem(chip + o, chips), core)}, device_id_type=MESH,
        )

    def end_copy(f, source_chip, target_chip):
        o = (target_chip - source_chip) % chips
        source = lat_of(source_chip, core)
        return pltpu.make_async_remote_copy(
            src_ref=chunk(f, source), dst_ref=chunk(f, source),
            send_sem=end_send.at[f, 0 if source_chip == 0 else 1], recv_sem=lane_recv.at[f, o],
            device_id={"lat": lat_of(target_chip, core)}, device_id_type=MESH,
        )

    def pair_copy(f, o):
        source = lat_of(lax.rem(chip + chips - o, chips), core)
        return pltpu.make_async_remote_copy(
            src_ref=chunk(f, source), dst_ref=chunk(f, source),
            send_sem=pair_send.at[f, o], recv_sem=pair_recv.at[f, o],
            device_id={"lat": lat_of(chip, 1 - core)}, device_id_type=MESH,
        )

    def pair_arrival(f, o):
        source = lat_of(lax.rem(chip + chips - o, chips), 1 - core)
        return pltpu.make_async_remote_copy(
            src_ref=chunk(f, source), dst_ref=chunk(f, source),
            send_sem=pair_send.at[f, o], recv_sem=pair_recv.at[f, o],
            device_id={"lat": lat_of(chip, 1 - core)}, device_id_type=MESH,
        )

    def slab_copy(f):
        return pltpu.make_async_remote_copy(
            src_ref=out_ref.at[:, pl.ds(f * front, front)], dst_ref=chunk(f, lat),
            send_sem=slab_send.at[f], recv_sem=slab_recv.at[f],
            device_id={"slab": lax.rem(slab + 1, n_slab)}, device_id_type=MESH,
        )

    relayed = chips > 2

    def direct(o):
        if not relayed:
            return True
        if o == chips - 1 and o == 1:
            return True
        if o == chips - 1:
            return chip != 0
        if o == 1:
            return chip != chips - 1
        return True

    def guarded(condition, action):
        if condition is True:
            action()
        else:
            pl.when(condition)(action)

    order = sorted(range(1, chips), key=lambda o: -min(o, chips - o))

    def distribute(f):
        @pl.when(first)
        def _():
            start_copy(f).wait()

        @pl.when(jnp.logical_not(first))
        def _():
            slab_copy(f).wait_recv()

        for o in order:
            guarded(direct(o), lambda o=o: lane_copy(f, o).start())
        pair_copy(f, 0).start()

    def hand_on(f):
        for o in order:
            lane_arrival(f, o).wait_recv()
            if relayed and o == chips - 2:
                @pl.when(chip == chips - 2)
                def _():
                    end_copy(f, 0, chips - 1).start()
            if relayed and o == 2:
                @pl.when(chip == 1)
                def _():
                    end_copy(f, chips - 1, 0).start()
            pair_copy(f, o).start()

    def compute(f):
        for o in range(chips):
            pair_arrival(f, o).wait_recv()
        positions = held.shape[1]
        for p in range(positions):
            high, low = halves(held[f, p])
            split[p, :front] = high
            split[p, front:] = low
        rows = pl.ds(pl.multiple_of(f * front, front), front)
        for j in range(blocks):
            picked = jnp.concatenate([split[cond[j, k]] for k in range(listed)], axis=1)
            product = jnp.dot(picked, weights[j], preferred_element_type=jnp.float32)
            out_ref[j, rows] += folded(product, front, size)

        @pl.when(jnp.logical_not(last))
        def _():
            slab_copy(f).start()

    @pl.when(first)
    def _():
        for f in range(min(LEAD, fronts)):
            distribute(f)

    for j in range(blocks):
        high, low = halves(noise_ref[j])
        left = jnp.concatenate([high, low], axis=0)
        high, low = halves(chol_ref[j].T)
        right = jnp.concatenate([high, low], axis=1)
        product = jnp.dot(left, right, preferred_element_type=jnp.float32)
        out_ref[j] = folded(product, nreal, size)

    for j in range(blocks):
        factor_copy(j).wait()

        @pl.loop(0, listed)
        def _(k):
            at = pl.multiple_of(k * size, size)
            high, low = halves(factors[j, :, pl.ds(at, size)].T)
            weights[j, pl.ds(at, size), :size] = high
            weights[j, pl.ds(at, size), size:] = low

    @pl.loop(0, fronts + 1)
    def _(i):
        @pl.when(jnp.logical_and(jnp.logical_not(first), i < fronts))
        def _():
            distribute(i)

        @pl.when(i < fronts)
        def _():
            hand_on(i)

        @pl.when(jnp.logical_and(first, i + LEAD < fronts))
        def _():
            distribute(i + LEAD)

        f = jnp.where(first, i, i - 1)

        @pl.when(jnp.logical_and(f >= 0, f < fronts))
        def _():
            compute(f)

    @pl.loop(0, fronts)
    def _(f):
        for o in range(1, chips):
            guarded(direct(o), lambda o=o: lane_copy(f, o).wait_send())
        for o in range(chips):
            pair_copy(f, o).wait_send()
        if relayed:
            @pl.when(chip == chips - 2)
            def _():
                end_copy(f, 0, chips - 1).wait_send()

            @pl.when(chip == 1)
            def _():
                end_copy(f, chips - 1, 0).wait_send()

        @pl.when(jnp.logical_not(last))
        def _():
            slab_copy(f).wait_send()


def solution(mesh):
    n_slab, n_lat = mesh.shape["slab"], mesh.shape["lat"]
    in_specs = (
        P(("slab", "lat"), None),
        P(("slab", "lat"), None, None),
        P(("slab", "lat"), None, None),
        P(("grp", "slab", "lat"), None, None),
        P(("grp", "lat"), None, None),
    )
    out_specs = P(("grp", "slab", "lat"), None, None)

    def shards(cond_lists, regress, chol, noise, start_field):
        blocks, nreal, size = noise.shape
        width = regress.shape[2]
        positions = blocks * n_lat
        front = min(FRONT, nreal)
        fronts = nreal // front
        chips = n_lat // 2
        vmem = pl.BlockSpec(memory_space=pltpu.VMEM)
        hbm = pl.BlockSpec(memory_space=pl.ANY)
        dma = pltpu.SemaphoreType.DMA
        return pl.pallas_call(
            functools.partial(kernel, n_slab, n_lat, front),
            out_shape=jax.ShapeDtypeStruct(noise.shape, jnp.float32),
            in_specs=[pl.BlockSpec(memory_space=pltpu.SMEM), hbm, vmem, vmem, hbm],
            out_specs=vmem,
            scratch_shapes=[
                pltpu.VMEM((fronts, positions, front, size), jnp.float32),
                pltpu.VMEM((blocks, size, width), jnp.float32),
                pltpu.VMEM((blocks, width, 2 * size), jnp.bfloat16),
                pltpu.VMEM((positions, 2 * front, size), jnp.bfloat16),
                dma((fronts,)),
                dma((blocks,)),
                dma((fronts, chips)),
                dma((fronts, chips)),
                dma((fronts, 2)),
                dma((fronts, chips)),
                dma((fronts, chips)),
                dma((fronts,)),
                dma((fronts,)),
            ],
            compiler_params=pltpu.CompilerParams(
                collective_id=0, has_side_effects=True, vmem_limit_bytes=48 * 1024 * 1024
            ),
            name="evolve",
        )(cond_lists, regress, chol, noise, start_field)

    return jax.shard_map(shards, mesh=mesh, in_specs=in_specs, out_specs=out_specs, check_vma=False)
```

```python
import functools

import jax
import jax.numpy as jnp
from jax import lax
from jax.experimental import pallas as pl
from jax.experimental.pallas import tpu as pltpu
from jax.sharding import PartitionSpec as P

MESH = pl.DeviceIdType.MESH
FRONT = 64
LEAD = 1


def halves(x):
    high = x.astype(jnp.bfloat16)
    low = (x - high.astype(jnp.float32)).astype(jnp.bfloat16)
    return high, low


def folded(product, rows, columns):
    small = product[:rows, columns:] + product[rows:, :columns] + product[rows:, columns:]
    return product[:rows, :columns] + small


def kernel(
    n_slab, n_lat, front,
    cond, regress_hbm, chol_ref, noise_ref, start_hbm, out_ref,
    held, factors, weights, split,
    start_sem, factor_sem,
    lane_send, lane_recv, end_send, pair_send, pair_recv, slab_send, slab_recv,
):
    blocks, nreal, size = noise_ref.shape
    listed = regress_hbm.shape[2] // size
    fronts = nreal // front
    chips = n_lat // 2
    slab = lax.axis_index("slab")
    lat = lax.axis_index("lat")
    chip, core = lax.div(lat, 2), lax.rem(lat, 2)
    first, last = slab == 0, slab == n_slab - 1

    def lat_of(other_chip, other_core):
        return other_chip * 2 + other_core

    def chunk(f, of_lat):
        return held.at[f, pl.ds(of_lat * blocks, blocks)]

    def start_copy(f):
        return pltpu.make_async_copy(
            start_hbm.at[:, pl.ds(f * front, front)], chunk(f, lat), start_sem.at[f]
        )

    def factor_copy(j):
        return pltpu.make_async_copy(regress_hbm.at[j], factors.at[j], factor_sem.at[j])

    @pl.when(first)
    def _():
        for f in range(fronts):
            start_copy(f).start()

    for j in range(blocks):
        factor_copy(j).start()

    barrier = pltpu.get_barrier_semaphore()

    def greet(**where):
        pl.semaphore_signal(barrier, inc=1, device_id=where, device_id_type=MESH)

    for o in range(1, chips):
        greet(lat=lat_of(lax.rem(chip + o, chips), core))
    greet(lat=lat_of(chip, 1 - core))

    @pl.when(jnp.logical_not(first))
    def _():
        greet(slab=slab - 1)

    @pl.when(jnp.logical_not(last))
    def _():
        greet(slab=slab + 1)

    partners = chips + jnp.where(first, 0, 1) + jnp.where(last, 0, 1)
    pl.semaphore_wait(barrier, partners)

    def lane_copy(f, o):
        return pltpu.make_async_remote_copy(
            src_ref=chunk(f, lat), dst_ref=chunk(f, lat),
            send_sem=lane_send.at[f, o], recv_sem=lane_recv.at[f, o],
            device_id={"lat": lat_of(lax.rem(chip + o, chips), core)}, device_id_type=MESH,
        )

    def lane_arrival(f, o):
        source = lat_of(lax.rem(chip + chips - o, chips), core)
        return pltpu.make_async_remote_copy(
            src_ref=chunk(f, source), dst_ref=chunk(f, source),
            send_sem=lane_send.at[f, o], recv_sem=lane_recv.at[f, o],
            device_id={"lat": lat_of(lax.rem(chip + o, chips), core)}, device_id_type=MESH,
        )

    def end_copy(f, source_chip, target_chip):
        o = (target_chip - source_chip) % chips
        source = lat_of(source_chip, core)
        return pltpu.make_async_remote_copy(
            src_ref=chunk(f, source), dst_ref=chunk(f, source),
            send_sem=end_send.at[f, 0 if source_chip == 0 else 1], recv_sem=lane_recv.at[f, o],
            device_id={"lat": lat_of(target_chip, core)}, device_id_type=MESH,
        )

    def pair_copy(f, o):
        source = lat_of(lax.rem(chip + chips - o, chips), core)
        return pltpu.make_async_remote_copy(
            src_ref=chunk(f, source), dst_ref=chunk(f, source),
            send_sem=pair_send.at[f, o], recv_sem=pair_recv.at[f, o],
            device_id={"lat": lat_of(chip, 1 - core)}, device_id_type=MESH,
        )

    def pair_arrival(f, o):
        source = lat_of(lax.rem(chip + chips - o, chips), 1 - core)
        return pltpu.make_async_remote_copy(
            src_ref=chunk(f, source), dst_ref=chunk(f, source),
            send_sem=pair_send.at[f, o], recv_sem=pair_recv.at[f, o],
            device_id={"lat": lat_of(chip, 1 - core)}, device_id_type=MESH,
        )

    def slab_copy(f):
        return pltpu.make_async_remote_copy(
            src_ref=out_ref.at[:, pl.ds(f * front, front)], dst_ref=chunk(f, lat),
            send_sem=slab_send.at[f], recv_sem=slab_recv.at[f],
            device_id={"slab": lax.rem(slab + 1, n_slab)}, device_id_type=MESH,
        )

    relayed = chips > 2

    def direct(o):
        if not relayed:
            return True
        if o == chips - 1 and o == 1:
            return True
        if o == chips - 1:
            return chip != 0
        if o == 1:
            return chip != chips - 1
        return True

    def guarded(condition, action):
        if condition is True:
            action()
        else:
            pl.when(condition)(action)

    order = sorted(range(1, chips), key=lambda o: -min(o, chips - o))

    def distribute(f):
        @pl.when(first)
        def _():
            start_copy(f).wait()

        @pl.when(jnp.logical_not(first))
        def _():
            slab_copy(f).wait_recv()

        for o in order:
            guarded(direct(o), lambda o=o: lane_copy(f, o).start())
        pair_copy(f, 0).start()

    def hand_on(f):
        for o in order:
            lane_arrival(f, o).wait_recv()
            if relayed and o == chips - 2:
                @pl.when(chip == chips - 2)
                def _():
                    end_copy(f, 0, chips - 1).start()
            if relayed and o == 2:
                @pl.when(chip == 1)
                def _():
                    end_copy(f, chips - 1, 0).start()
            pair_copy(f, o).start()

    def compute(f):
        for o in range(chips):
            pair_arrival(f, o).wait_recv()
        positions = held.shape[1]
        for p in range(positions):
            high, low = halves(held[f, p])
            split[p, :front] = high
            split[p, front:] = low
        rows = pl.ds(pl.multiple_of(f * front, front), front)
        for j in range(blocks):
            picked = jnp.concatenate([split[cond[j, k]] for k in range(listed)], axis=1)
            product = jnp.dot(picked, weights[j], preferred_element_type=jnp.float32)
            out_ref[j, rows] += folded(product, front, size)

        @pl.when(jnp.logical_not(last))
        def _():
            slab_copy(f).start()

    @pl.when(first)
    def _():
        for f in range(min(LEAD, fronts)):
            distribute(f)

    for j in range(blocks):
        high, low = halves(noise_ref[j])
        left = jnp.concatenate([high, low], axis=0)
        high, low = halves(chol_ref[j].T)
        right = jnp.concatenate([high, low], axis=1)
        product = jnp.dot(left, right, preferred_element_type=jnp.float32)
        out_ref[j] = folded(product, nreal, size)

    for j in range(blocks):
        factor_copy(j).wait()

        @pl.loop(0, listed)
        def _(k):
            at = pl.multiple_of(k * size, size)
            high, low = halves(factors[j, :, pl.ds(at, size)].T)
            weights[j, pl.ds(at, size), :size] = high
            weights[j, pl.ds(at, size), size:] = low

    @pl.loop(0, fronts + 1)
    def _(i):
        @pl.when(jnp.logical_and(jnp.logical_not(first), i < fronts))
        def _():
            distribute(i)

        @pl.when(i < fronts)
        def _():
            hand_on(i)

        @pl.when(jnp.logical_and(first, i + LEAD < fronts))
        def _():
            distribute(i + LEAD)

        f = jnp.where(first, i, i - 1)

        @pl.when(jnp.logical_and(f >= 0, f < fronts))
        def _():
            compute(f)

    @pl.loop(0, fronts)
    def _(f):
        for o in range(1, chips):
            guarded(direct(o), lambda o=o: lane_copy(f, o).wait_send())
        for o in range(chips):
            pair_copy(f, o).wait_send()
        if relayed:
            @pl.when(chip == chips - 2)
            def _():
                end_copy(f, 0, chips - 1).wait_send()

            @pl.when(chip == 1)
            def _():
                end_copy(f, chips - 1, 0).wait_send()

        @pl.when(jnp.logical_not(last))
        def _():
            slab_copy(f).wait_send()


def solution(mesh):
    n_slab, n_lat = mesh.shape["slab"], mesh.shape["lat"]
    in_specs = (
        P(("slab", "lat"), None),
        P(("slab", "lat"), None, None),
        P(("slab", "lat"), None, None),
        P(("grp", "slab", "lat"), None, None),
        P(("grp", "lat"), None, None),
    )
    out_specs = P(("grp", "slab", "lat"), None, None)

    def shards(cond_lists, regress, chol, noise, start_field):
        blocks, nreal, size = noise.shape
        width = regress.shape[2]
        positions = blocks * n_lat
        front = min(FRONT, nreal)
        fronts = nreal // front
        chips = n_lat // 2
        vmem = pl.BlockSpec(memory_space=pltpu.VMEM)
        hbm = pl.BlockSpec(memory_space=pl.ANY)
        dma = pltpu.SemaphoreType.DMA
        return pl.pallas_call(
            functools.partial(kernel, n_slab, n_lat, front),
            out_shape=jax.ShapeDtypeStruct(noise.shape, jnp.float32),
            in_specs=[pl.BlockSpec(memory_space=pltpu.SMEM), hbm, vmem, vmem, hbm],
            out_specs=vmem,
            scratch_shapes=[
                pltpu.VMEM((fronts, positions, front, size), jnp.float32),
                pltpu.VMEM((blocks, size, width), jnp.float32),
                pltpu.VMEM((blocks, width, 2 * size), jnp.bfloat16),
                pltpu.VMEM((positions, 2 * front, size), jnp.bfloat16),
                dma((fronts,)),
                dma((blocks,)),
                dma((fronts, chips)),
                dma((fronts, chips)),
                dma((fronts, 2)),
                dma((fronts, chips)),
                dma((fronts, chips)),
                dma((fronts,)),
                dma((fronts,)),
            ],
            compiler_params=pltpu.CompilerParams(
                collective_id=0, has_side_effects=True, vmem_limit_bytes=48 * 1024 * 1024
            ),
            name="evolve",
        )(cond_lists, regress, chol, noise, start_field)

    return jax.shard_map(shards, mesh=mesh, in_specs=in_specs, out_specs=out_specs, check_vma=False)
```

```python
import functools

import jax
import jax.numpy as jnp
from jax import lax
from jax.experimental import pallas as pl
from jax.experimental.pallas import tpu as pltpu
from jax.sharding import PartitionSpec as P

MESH = pl.DeviceIdType.MESH
FRONT = 64
LEAD = 1


def halves(x):
    high = x.astype(jnp.bfloat16)
    low = (x - high.astype(jnp.float32)).astype(jnp.bfloat16)
    return high, low


def folded(product, rows, columns):
    small = product[:rows, columns:] + product[rows:, :columns] + product[rows:, columns:]
    return product[:rows, :columns] + small


def kernel(
    n_slab, n_lat, front,
    cond, regress_hbm, chol_ref, noise_ref, start_hbm, out_ref,
    held, factors, weights, split,
    start_sem, factor_sem,
    lane_send, lane_recv, end_send, pair_send, pair_recv, slab_send, slab_recv,
):
    blocks, nreal, size = noise_ref.shape
    listed = regress_hbm.shape[2] // size
    fronts = nreal // front
    chips = n_lat // 2
    slab = lax.axis_index("slab")
    lat = lax.axis_index("lat")
    chip, core = lax.div(lat, 2), lax.rem(lat, 2)
    first, last = slab == 0, slab == n_slab - 1

    def lat_of(other_chip, other_core):
        return other_chip * 2 + other_core

    def chunk(f, of_lat):
        return held.at[f, pl.ds(of_lat * blocks, blocks)]

    def start_copy(f):
        return pltpu.make_async_copy(
            start_hbm.at[:, pl.ds(f * front, front)], chunk(f, lat), start_sem.at[f]
        )

    def factor_copy(j):
        return pltpu.make_async_copy(regress_hbm.at[j], factors.at[j], factor_sem.at[j])

    @pl.when(first)
    def _():
        for f in range(fronts):
            start_copy(f).start()

    for j in range(blocks):
        factor_copy(j).start()

    barrier = pltpu.get_barrier_semaphore()

    def greet(**where):
        pl.semaphore_signal(barrier, inc=1, device_id=where, device_id_type=MESH)

    for o in range(1, chips):
        greet(lat=lat_of(lax.rem(chip + o, chips), core))
    greet(lat=lat_of(chip, 1 - core))

    @pl.when(jnp.logical_not(first))
    def _():
        greet(slab=slab - 1)

    @pl.when(jnp.logical_not(last))
    def _():
        greet(slab=slab + 1)

    partners = chips + jnp.where(first, 0, 1) + jnp.where(last, 0, 1)
    pl.semaphore_wait(barrier, partners)

    def lane_copy(f, o):
        return pltpu.make_async_remote_copy(
            src_ref=chunk(f, lat), dst_ref=chunk(f, lat),
            send_sem=lane_send.at[f, o], recv_sem=lane_recv.at[f, o],
            device_id={"lat": lat_of(lax.rem(chip + o, chips), core)}, device_id_type=MESH,
        )

    def lane_arrival(f, o):
        source = lat_of(lax.rem(chip + chips - o, chips), core)
        return pltpu.make_async_remote_copy(
            src_ref=chunk(f, source), dst_ref=chunk(f, source),
            send_sem=lane_send.at[f, o], recv_sem=lane_recv.at[f, o],
            device_id={"lat": lat_of(lax.rem(chip + o, chips), core)}, device_id_type=MESH,
        )

    def end_copy(f, source_chip, target_chip):
        o = (target_chip - source_chip) % chips
        source = lat_of(source_chip, core)
        return pltpu.make_async_remote_copy(
            src_ref=chunk(f, source), dst_ref=chunk(f, source),
            send_sem=end_send.at[f, 0 if source_chip == 0 else 1], recv_sem=lane_recv.at[f, o],
            device_id={"lat": lat_of(target_chip, core)}, device_id_type=MESH,
        )

    def pair_copy(f, o):
        source = lat_of(lax.rem(chip + chips - o, chips), core)
        return pltpu.make_async_remote_copy(
            src_ref=chunk(f, source), dst_ref=chunk(f, source),
            send_sem=pair_send.at[f, o], recv_sem=pair_recv.at[f, o],
            device_id={"lat": lat_of(chip, 1 - core)}, device_id_type=MESH,
        )

    def pair_arrival(f, o):
        source = lat_of(lax.rem(chip + chips - o, chips), 1 - core)
        return pltpu.make_async_remote_copy(
            src_ref=chunk(f, source), dst_ref=chunk(f, source),
            send_sem=pair_send.at[f, o], recv_sem=pair_recv.at[f, o],
            device_id={"lat": lat_of(chip, 1 - core)}, device_id_type=MESH,
        )

    def slab_copy(f):
        return pltpu.make_async_remote_copy(
            src_ref=out_ref.at[:, pl.ds(f * front, front)], dst_ref=chunk(f, lat),
            send_sem=slab_send.at[f], recv_sem=slab_recv.at[f],
            device_id={"slab": lax.rem(slab + 1, n_slab)}, device_id_type=MESH,
        )

    relayed = chips > 2

    def direct(o):
        if not relayed:
            return True
        if o == chips - 1 and o == 1:
            return True
        if o == chips - 1:
            return chip != 0
        if o == 1:
            return chip != chips - 1
        return True

    def guarded(condition, action):
        if condition is True:
            action()
        else:
            pl.when(condition)(action)

    order = sorted(range(1, chips), key=lambda o: -min(o, chips - o))

    def distribute(f):
        @pl.when(first)
        def _():
            start_copy(f).wait()

        @pl.when(jnp.logical_not(first))
        def _():
            slab_copy(f).wait_recv()

        for o in order:
            guarded(direct(o), lambda o=o: lane_copy(f, o).start())
        pair_copy(f, 0).start()

    relays = [o for o in order if relayed and o in (2, chips - 2)]

    def hand_on(f):
        for o in relays:
            lane_arrival(f, o).wait_recv()
            if o == chips - 2:
                @pl.when(chip == chips - 2)
                def _():
                    end_copy(f, 0, chips - 1).start()
            if o == 2:
                @pl.when(chip == 1)
                def _():
                    end_copy(f, chips - 1, 0).start()
            pair_copy(f, o).start()

    def share(f):
        for o in order:
            if o not in relays:
                lane_arrival(f, o).wait_recv()
                pair_copy(f, o).start()

    def compute(f):
        for o in range(chips):
            pair_arrival(f, o).wait_recv()
        positions = held.shape[1]
        for p in range(positions):
            high, low = halves(held[f, p])
            split[p, :front] = high
            split[p, front:] = low
        rows = pl.ds(pl.multiple_of(f * front, front), front)
        for j in range(blocks):
            picked = jnp.concatenate([split[cond[j, k]] for k in range(listed)], axis=1)
            product = jnp.dot(picked, weights[j], preferred_element_type=jnp.float32)
            out_ref[j, rows] += folded(product, front, size)

        @pl.when(jnp.logical_not(last))
        def _():
            slab_copy(f).start()

    @pl.when(first)
    def _():
        for f in range(min(LEAD, fronts)):
            distribute(f)

    for j in range(blocks):
        high, low = halves(noise_ref[j])
        left = jnp.concatenate([high, low], axis=0)
        high, low = halves(chol_ref[j].T)
        right = jnp.concatenate([high, low], axis=1)
        product = jnp.dot(left, right, preferred_element_type=jnp.float32)
        out_ref[j] = folded(product, nreal, size)

    for j in range(blocks):
        factor_copy(j).wait()

        @pl.loop(0, listed)
        def _(k):
            at = pl.multiple_of(k * size, size)
            high, low = halves(factors[j, :, pl.ds(at, size)].T)
            weights[j, pl.ds(at, size), :size] = high
            weights[j, pl.ds(at, size), size:] = low

    @pl.loop(0, fronts + 1)
    def _(i):
        @pl.when(jnp.logical_and(jnp.logical_not(first), i < fronts))
        def _():
            distribute(i)

        @pl.when(i < fronts)
        def _():
            hand_on(i)

        @pl.when(jnp.logical_and(first, i + LEAD < fronts))
        def _():
            distribute(i + LEAD)

        f = jnp.where(first, i, i - 1)

        @pl.when(jnp.logical_and(f >= 0, f < fronts))
        def _():
            share(f)
            compute(f)

    @pl.loop(0, fronts)
    def _(f):
        for o in range(1, chips):
            guarded(direct(o), lambda o=o: lane_copy(f, o).wait_send())
        for o in range(chips):
            pair_copy(f, o).wait_send()
        if relayed:
            @pl.when(chip == chips - 2)
            def _():
                end_copy(f, 0, chips - 1).wait_send()

            @pl.when(chip == 1)
            def _():
                end_copy(f, chips - 1, 0).wait_send()

        @pl.when(jnp.logical_not(last))
        def _():
            slab_copy(f).wait_send()


def solution(mesh):
    n_slab, n_lat = mesh.shape["slab"], mesh.shape["lat"]
    in_specs = (
        P(("slab", "lat"), None),
        P(("slab", "lat"), None, None),
        P(("slab", "lat"), None, None),
        P(("grp", "slab", "lat"), None, None),
        P(("grp", "lat"), None, None),
    )
    out_specs = P(("grp", "slab", "lat"), None, None)

    def shards(cond_lists, regress, chol, noise, start_field):
        blocks, nreal, size = noise.shape
        width = regress.shape[2]
        positions = blocks * n_lat
        front = min(FRONT, nreal)
        fronts = nreal // front
        chips = n_lat // 2
        vmem = pl.BlockSpec(memory_space=pltpu.VMEM)
        hbm = pl.BlockSpec(memory_space=pl.ANY)
        dma = pltpu.SemaphoreType.DMA
        return pl.pallas_call(
            functools.partial(kernel, n_slab, n_lat, front),
            out_shape=jax.ShapeDtypeStruct(noise.shape, jnp.float32),
            in_specs=[pl.BlockSpec(memory_space=pltpu.SMEM), hbm, vmem, vmem, hbm],
            out_specs=vmem,
            scratch_shapes=[
                pltpu.VMEM((fronts, positions, front, size), jnp.float32),
                pltpu.VMEM((blocks, size, width), jnp.float32),
                pltpu.VMEM((blocks, width, 2 * size), jnp.bfloat16),
                pltpu.VMEM((positions, 2 * front, size), jnp.bfloat16),
                dma((fronts,)),
                dma((blocks,)),
                dma((fronts, chips)),
                dma((fronts, chips)),
                dma((fronts, 2)),
                dma((fronts, chips)),
                dma((fronts, chips)),
                dma((fronts,)),
                dma((fronts,)),
            ],
            compiler_params=pltpu.CompilerParams(
                collective_id=0, has_side_effects=True, vmem_limit_bytes=48 * 1024 * 1024
            ),
            name="evolve",
        )(cond_lists, regress, chol, noise, start_field)

    return jax.shard_map(shards, mesh=mesh, in_specs=in_specs, out_specs=out_specs, check_vma=False)
```
